512 devices in a mesh: pair: 64 (over x_lo, z, core), band: 8 (over x_hi, y).
Axes of the slice: x: 4 (x_hi: 2, x_lo: 2; x = x_hi * 2 + x_lo), y: 4, z: 16, core: 2. Of those that a mesh axis runs over, the one named last changes fastest.
Arguments:
- spectra: bfloat16 [64, 2, 384, 16384], P('band', None, None, 'pair'), may hold values from -1040 to 1040
- window_valid: int32 [384, 16384], P(None, 'pair'), may hold values 0 or 1
Outputs:
- correlation: bfloat16 [2, 32, 16384, 256], P(None, 'band', 'pair')
The draws below stay inside these ranges and needn't reach their ends.
All inputs are finite; a program needn't handle non-finite values. No bound on the sum of `window_valid` on one device may be relied on, other than what follows from the above.
Results may differ from the reference program's by a relative error of at most 0.0067.
Values may be sent and summed in bfloat16 or wider, within the bound.
No kernel may reach another device: no remote copies, remote signals or barrier semaphores. Data moves between devices by JAX's collectives and lax.ppermute only.
A program may use at most 64 MiB of HBM per device.

```python
import math
import jax
import jax.numpy as jnp
from jax import lax

FREQS = 64
BLOCK = 256
WIN = 384
ROUNDS = 2
NBLOCKS = 64
CHANNELS = 16384
KEEP = 32


def draw_spectra(key, part):
    key = jax.random.fold_in(key, 17)
    key_bins, key_rows, key_values = jax.random.split(key, 3)
    bin_index = jnp.arange(FREQS, dtype=jnp.float32)
    bin_trend = jnp.sqrt(1.0 + 2.0 * bin_index / (FREQS - 1))
    roughness = jnp.exp(jax.random.uniform(key_bins, (FREQS,), jnp.float32, 0.0, math.log(10.0)))
    bin_scale = bin_trend * roughness
    row_scale = jnp.exp(jax.random.uniform(key_rows, (WIN, CHANNELS), jnp.float32, 0.0, math.log(10.0)))
    values = jnp.clip(jax.random.normal(key_values, (FREQS, 2, WIN, CHANNELS), jnp.float32), -6.0, 6.0)
    return (values * bin_scale[:, None, None, None] * row_scale[None, None]).astype(jnp.bfloat16)


def plant(drawn, stream_key, least, top_value):
    longest = drawn.shape.index(max(drawn.shape))
    spots = []
    for shift in (0, 1):
        where = [jax.random.randint(jax.random.fold_in(stream_key, axis), (), 0, length) for axis, length in enumerate(drawn.shape)]
        where[longest] = (where[longest] + shift) % drawn.shape[longest]
        spots.append(tuple(where))
    return drawn.at[spots[0]].set(least).at[spots[1]].set(top_value)


def setup_inputs(seed: int = 0) -> dict:
    key_of = jax.random.split(jax.random.key(seed), 3)
    spectra = draw_spectra(jax.random.fold_in(key_of[2], 71), 0)
    window_valid = plant((jax.random.randint(key_of[1], (WIN, CHANNELS), 0, 4) < 3).astype(jnp.int32), jax.random.fold_in(key_of[1], 1), 0, 1)
    return dict(spectra=spectra, window_valid=window_valid)


EPSILON = 1e-06

def whiten_block(spectra_block, valid_block):
    values = spectra_block.astype(jnp.float32)
    energy = lax.optimization_barrier(jnp.sum(values * values, axis=(0, 1))) / FREQS
    factor = valid_block.astype(jnp.float32) * lax.rsqrt(energy + EPSILON)
    return (values * factor[None, None]).astype(jnp.bfloat16)

def take_block(spectra, window_valid, block_index):
    start_col = (block_index * BLOCK).astype(jnp.int32)
    spectra_block = lax.dynamic_slice_in_dim(spectra, start_col, BLOCK, axis=3)
    valid_block = lax.dynamic_slice_in_dim(window_valid, start_col, BLOCK, axis=1)
    return whiten_block(spectra_block, valid_block)

def cross_spectra(own_white, partner):
    own_values = own_white.astype(jnp.float32)
    partner_values = partner.astype(jnp.float32)
    real_part = jnp.einsum('fwa,fwb->fab', own_values[:, 0], partner_values[:, 0]) + jnp.einsum('fwa,fwb->fab', own_values[:, 1], partner_values[:, 1])
    imag_part = jnp.einsum('fwa,fwb->fab', own_values[:, 0], partner_values[:, 1]) - jnp.einsum('fwa,fwb->fab', own_values[:, 1], partner_values[:, 0])
    return jnp.stack([real_part, imag_part], axis=2).astype(jnp.bfloat16)

def lag_table():
    lag_index = jnp.arange(KEEP, dtype=jnp.float32) - KEEP // 2
    bin_index = jnp.arange(FREQS, dtype=jnp.float32) + 1.0
    phase_angle = 2.0 * math.pi / (2 * FREQS) * lag_index[:, None] * bin_index[None, :]
    return jnp.stack([jnp.cos(phase_angle), -jnp.sin(phase_angle)], axis=2).astype(jnp.bfloat16)

def to_lags(cross_block):
    lagged = jnp.einsum('jfp,fapb->jab', lag_table().astype(jnp.float32), cross_block.astype(jnp.float32))
    return (lagged * (1.0 / math.sqrt(FREQS * WIN))).astype(jnp.bfloat16)

def reference(spectra, window_valid):

    def one_block(block_index):
        own_white = take_block(spectra, window_valid, block_index)
        results = []
        for distance in range(1, ROUNDS + 1):
            partner = take_block(spectra, window_valid, (block_index + distance) % NBLOCKS)
            results.append(to_lags(cross_spectra(own_white, partner)))
        return jnp.stack(results)
    stacked = lax.map(one_block, jnp.arange(NBLOCKS, dtype=jnp.int32))
    ordered = jnp.transpose(stacked, (1, 2, 0, 3, 4))
    return ordered.reshape(ROUNDS, KEEP, NBLOCKS * BLOCK, BLOCK)
```

```python
import math

import jax
import jax.numpy as jnp
import numpy as np
from jax import lax
from jax.experimental import pallas as pl
from jax.experimental.pallas import tpu as pltpu
from jax.sharding import PartitionSpec as P

FREQS = 64
KEEP = 32
WIN = 384
EPSILON = 1e-06
HALF = 128
SUB = 16
VMEM_LIMIT = 48 * 1024 * 1024

BF16 = jnp.bfloat16
F32 = jnp.float32


def params():
    return pltpu.CompilerParams(vmem_limit_bytes=VMEM_LIMIT)


def lag_matrix():
    lag_index = np.arange(KEEP, dtype=np.float32) - np.float32(KEEP // 2)
    bin_index = np.arange(FREQS, dtype=np.float32) + np.float32(1.0)
    step = np.float32(2.0 * math.pi / (2 * FREQS))
    phase = (step * lag_index)[:, None] * bin_index[None, :]
    table = np.stack([np.cos(phase), -np.sin(phase)], axis=2).reshape(KEEP, 2 * FREQS)
    return jnp.asarray(np.kron(table, np.eye(SUB, dtype=np.float32)), dtype=BF16)


def whiten(raw, factor):
    return (raw.astype(F32) * factor.astype(F32)[None]).astype(BF16)


def product(left, right):
    windows = left.shape[1]
    rows = left.reshape(2 * windows, left.shape[2])
    top = jnp.concatenate([right[0], right[1]], axis=1)
    low = jnp.concatenate([right[1], -right[0]], axis=1)
    cols = jnp.concatenate([top, low], axis=0)
    return lax.dot_general(rows, cols, (((0,), (0,)), ((), ())), preferred_element_type=F32)


def store_tall(out_ref, result):
    for part in range(2):
        piece = result[:, part * HALF : (part + 1) * HALF]
        out_ref[:, part] = piece.astype(BF16).reshape(8, 32, HALF)


def store_wide(out_ref, result):
    for part in range(2):
        for half in range(2):
            start = part * 2 * HALF + half * HALF
            piece = result[:, start : start + HALF]
            out_ref[half * 4 : half * 4 + 4, part] = piece.astype(BF16).reshape(4, 32, HALF)


def early_kernel(odd_ref, s_ref, t_ref, fs_ref, ft_ref, sw_ref, tw_ref, out_ref):
    sw_ref[0] = whiten(s_ref[0], fs_ref[...])
    tw_ref[0] = whiten(t_ref[0], ft_ref[...])

    @pl.when(odd_ref[0] == 0)
    def _():
        store_tall(out_ref, product(sw_ref[0], tw_ref[0, :, :, :HALF]))

    @pl.when(odd_ref[0] != 0)
    def _():
        store_tall(out_ref, product(tw_ref[0], sw_ref[0, :, :, HALF:]))


def first_kernel(odd_ref, s_ref, u_ref, fu_ref, uw_ref, out_ref):
    uw_ref[0] = whiten(u_ref[0], fu_ref[...])

    @pl.when(odd_ref[0] == 0)
    def _():
        store_tall(out_ref, product(s_ref[0], uw_ref[0]))

    @pl.when(odd_ref[0] != 0)
    def _():
        store_wide(out_ref, product(uw_ref[0], s_ref[0]))


def second_kernel(odd_ref, s_ref, t_ref, u_ref, fu_ref, v_ref, out_ref, mid_ref):
    uw = whiten(u_ref[0], fu_ref[...])

    @pl.when(odd_ref[0] == 0)
    def _():
        store_tall(out_ref, product(s_ref[0], uw))
        store_tall(mid_ref, product(t_ref[0], uw))

    @pl.when(odd_ref[0] != 0)
    def _():
        store_wide(out_ref, product(uw, s_ref[0]))
        store_tall(mid_ref, product(s_ref[0], v_ref[0]))


def bin_spec(channels):
    return pl.BlockSpec((1, 2, WIN, channels), lambda f: (f, 0, 0, 0))


def factor_spec(channels):
    return pl.BlockSpec((WIN, channels), lambda f: (0, 0))


def flag_spec():
    return pl.BlockSpec(memory_space=pltpu.SMEM)


def send_spec():
    return pl.BlockSpec((8, 2, 32, HALF), lambda f: (0, f, 0, 0))


SEND = jax.ShapeDtypeStruct((8, 16, 32, HALF), BF16)


def cost(products, nbytes):
    return pl.CostEstimate(
        flops=int(products * 2 * 8 * 768 * 256 * 256), bytes_accessed=int(nbytes), transcendentals=0
    )


def early(odd, s, t, fs, ft):
    whole = jax.ShapeDtypeStruct(s.shape, BF16)
    return pl.pallas_call(
        early_kernel,
        grid=(8,),
        in_specs=[flag_spec(), bin_spec(256), bin_spec(256), factor_spec(256), factor_spec(256)],
        out_specs=[bin_spec(256), bin_spec(256), send_spec()],
        out_shape=[whole, whole, SEND],
        compiler_params=params(),
        cost_estimate=cost(1, 13 << 20),
        name="early",
    )(odd, s, t, fs, ft)


def first(odd, sw, u, fu):
    return pl.pallas_call(
        first_kernel,
        grid=(8,),
        in_specs=[flag_spec(), bin_spec(256), bin_spec(HALF), factor_spec(HALF)],
        out_specs=[bin_spec(HALF), send_spec()],
        out_shape=[jax.ShapeDtypeStruct(u.shape, BF16), SEND],
        compiler_params=params(),
        cost_estimate=cost(1, 7 << 20),
        name="first",
    )(odd, sw, u, fu)


def second(odd, sw, tw, u, fu, vw):
    return pl.pallas_call(
        second_kernel,
        grid=(8,),
        in_specs=[flag_spec(), bin_spec(256), bin_spec(256), bin_spec(HALF), factor_spec(HALF), bin_spec(HALF)],
        out_specs=[send_spec(), send_spec()],
        out_shape=[SEND, SEND],
        compiler_params=params(),
        cost_estimate=cost(2, 11 << 20),
        name="second",
    )(odd, sw, tw, u, fu, vw)


def lags_kernel(scale, matrix_ref, cross_ref, out_ref):
    cross = cross_ref[...].reshape(2 * FREQS, 32, HALF)
    pair = jnp.concatenate([cross[:, :SUB], cross[:, SUB:]], axis=2)
    lagged = lax.dot_general(
        matrix_ref[...],
        pair.reshape(2 * FREQS * SUB, 2 * HALF),
        (((1,), (0,)), ((), ())),
        preferred_element_type=F32,
    )
    lagged = (lagged * scale).astype(BF16)
    for half in range(2):
        piece = lagged[:, half * HALF : (half + 1) * HALF].reshape(8, 4, SUB, HALF)
        out_ref[:, :, half * SUB : (half + 1) * SUB] = piece


def to_lags(matrix, cross, scale):
    def kernel(matrix_ref, cross_ref, out_ref):
        lags_kernel(scale, matrix_ref, cross_ref, out_ref)

    return pl.pallas_call(
        kernel,
        in_specs=[pl.BlockSpec(memory_space=pltpu.VMEM)] * 2,
        out_specs=pl.BlockSpec(memory_space=pltpu.VMEM),
        out_shape=jax.ShapeDtypeStruct((8, 4, 32, HALF), BF16),
        compiler_params=params(),
        cost_estimate=pl.CostEstimate(
            flops=2 * 512 * 2048 * 256, bytes_accessed=4 << 20, transcendentals=0
        ),
        name="to_lags",
    )(matrix, cross)


def assemble_kernel(odd_ref, own_ref, got_ref, x0_ref, x1_ref, out_ref):
    for src in range(8):
        rows = slice(src * 32, src * 32 + 32)
        out_ref[0, :, rows, :HALF] = own_ref[src]
        out_ref[0, :, rows, HALF:] = got_ref[src]

    @pl.when(odd_ref[0] == 0)
    def _():
        for src in range(8):
            rows = slice(src * 32, src * 32 + 32)
            out_ref[1, :, rows, :HALF] = x0_ref[src]
            out_ref[1, :, rows, HALF:] = x1_ref[src]

    @pl.when(odd_ref[0] != 0)
    def _():
        for index, ref in enumerate((x0_ref, x1_ref)):
            for src in range(8):
                half, row = src // 4, index * HALF + (src % 4) * 32
                out_ref[1, :, row : row + 32, half * HALF : (half + 1) * HALF] = ref[src]


def assemble(odd, own, got, x0, x1):
    return pl.pallas_call(
        assemble_kernel,
        in_specs=[flag_spec()] + [pl.BlockSpec(memory_space=pltpu.VMEM)] * 4,
        out_specs=pl.BlockSpec(memory_space=pltpu.VMEM),
        out_shape=jax.ShapeDtypeStruct((2, 4, 256, 256), BF16),
        compiler_params=params(),
        cost_estimate=pl.CostEstimate(flops=0, bytes_accessed=2 << 20, transcendentals=0),
        name="assemble",
    )(odd, own, got, x0, x1)


def band_sum(value):
    exchanges = (lambda b: b ^ 1, lambda b: (b // 4) * 4 + 3 - b % 4, lambda b: (b + 4) % 8)
    for partner in exchanges:
        route = [(b, partner(b)) for b in range(8)]
        value = value + lax.ppermute(value.astype(BF16), "band", route).astype(F32)
    return value


def regroup(block):
    return lax.all_to_all(block, "band", split_axis=0, concat_axis=0, tiled=True)


def shards(spectra, window_valid):
    blocks = lax.axis_size("pair")
    odd = lax.axis_index("pair") % 2
    flag = odd.astype(jnp.int32).reshape(1)
    across = [((p + 2) % blocks, p) if p % 2 == 0 else ((p - 2) % blocks, p) for p in range(blocks)]
    swap = [(p ^ 1, p) for p in range(blocks)]
    back = [(p, p) if p % 2 == 0 else ((p + 2) % blocks, p) for p in range(blocks)]

    u0 = lax.ppermute(spectra[..., :HALF], "pair", across)
    t = lax.ppermute(spectra, "pair", swap)
    u1 = lax.ppermute(spectra[..., HALF:], "pair", across)

    values = spectra.astype(F32)
    energy = band_sum(jnp.sum(values * values, axis=(0, 1)))
    fs = window_valid.astype(F32) * lax.rsqrt(energy / FREQS + EPSILON)
    fs16 = fs.astype(BF16)
    ft = lax.ppermute(fs16, "pair", swap)
    fu = lax.ppermute(fs16, "pair", across)

    matrix = lag_matrix()
    scale = 1.0 / math.sqrt(FREQS * WIN)

    sw, tw, cross_e = early(flag, spectra, t, fs, ft)
    got_e = regroup(cross_e)
    uw0, cross_f0 = first(flag, sw, u0, fu[:, :HALF])
    vw = lax.ppermute(uw0, "pair", swap)
    got_f0 = regroup(cross_f0)
    cross_f1, cross_g = second(flag, sw, tw, u1, fu[:, HALF:], vw)
    got_f1 = regroup(cross_f1)
    got_g = regroup(cross_g)

    lag_e = regroup(to_lags(matrix, got_e, scale))
    lag_f0 = lax.ppermute(regroup(to_lags(matrix, got_f0, scale)), "pair", back)
    lag_f1 = lax.ppermute(regroup(to_lags(matrix, got_f1, scale)), "pair", back)
    lag_g = regroup(to_lags(matrix, got_g, scale))
    own = jnp.where(odd == 0, lag_e, lag_g)
    got = lax.ppermute(jnp.where(odd == 0, lag_g, lag_e), "pair", swap)
    return assemble(flag, own, got, lag_f0, lag_f1)


def solution(mesh):
    return jax.shard_map(
        shards,
        mesh=mesh,
        in_specs=(P("band", None, None, "pair"), P(None, "pair")),
        out_specs=P(None, "band", "pair", None),
        check_vma=False,
    )
```

```python
import functools
import math

import jax
import jax.numpy as jnp
import numpy as np
from jax import lax
from jax.experimental import pallas as pl
from jax.experimental.pallas import tpu as pltpu
from jax.sharding import PartitionSpec as P

FREQS = 64
KEEP = 32
WIN = 384
EPSILON = 1e-06
BLOCK = 256
SUB = 16
VMEM_LIMIT = 28 * 1024 * 1024

BF16 = jnp.bfloat16
F32 = jnp.float32


def params():
    return pltpu.CompilerParams(vmem_limit_bytes=VMEM_LIMIT)


def lag_matrix(first, bins):
    lag_index = np.arange(KEEP, dtype=np.float32) - np.float32(KEEP // 2)
    bin_index = np.arange(FREQS, dtype=np.float32) + np.float32(1.0)
    step = np.float32(2.0 * math.pi / (2 * FREQS))
    phase = (step * lag_index)[:, None] * bin_index[None, :]
    table = np.stack([np.cos(phase), -np.sin(phase)], axis=2).reshape(KEEP, 8, 8, 2)
    table = table[:, :, first : first + bins].reshape(KEEP, 16 * bins)
    return jnp.asarray(np.kron(table, np.eye(SUB, dtype=np.float32)), dtype=BF16)


def whiten(raw, factor):
    return raw * factor[None]


def product(left, right):
    windows = left.shape[1]
    rows = left.reshape(2 * windows, left.shape[2])
    top = jnp.concatenate([right[0], right[1]], axis=1)
    low = jnp.concatenate([right[1], -right[0]], axis=1)
    cols = jnp.concatenate([top, low], axis=0)
    return lax.dot_general(rows, cols, (((0,), (0,)), ((), ())), preferred_element_type=F32)


def store(out_ref, result, start):
    for part in range(2):
        piece = result[:, part * BLOCK : (part + 1) * BLOCK]
        out_ref[:, part, :, start : start + BLOCK] = piece.astype(BF16).reshape(8, 32, BLOCK)


def cross_kernel(odd_ref, s_ref, n_ref, u_ref, fs_ref, fn_ref, fu_ref, out_ref):
    own = whiten(s_ref[0], fs_ref[...])
    near = whiten(n_ref[0], fn_ref[...])
    far = whiten(u_ref[0], fu_ref[...])

    @pl.when(odd_ref[0] == 0)
    def _():
        store(out_ref, product(near, far), 0)
        store(out_ref, product(own, far), BLOCK)

    @pl.when(odd_ref[0] != 0)
    def _():
        store(out_ref, product(near, own), 0)
        store(out_ref, product(far, own), BLOCK)


def flag_spec():
    return pl.BlockSpec(memory_space=pltpu.SMEM)


def held_spec():
    return pl.BlockSpec(memory_space=pltpu.VMEM)


def cross_spectra(first, odd, s, n, u, fs, fn, fu):
    bins = u.shape[0]
    factor = pl.BlockSpec((WIN, BLOCK), lambda f: (0, 0))
    shifted = pl.BlockSpec((1, 2, WIN, BLOCK), lambda f: (first + f, 0, 0, 0))
    plain = pl.BlockSpec((1, 2, WIN, BLOCK), lambda f: (f, 0, 0, 0))
    return pl.pallas_call(
        cross_kernel,
        grid=(bins,),
        in_specs=[flag_spec(), shifted, shifted, plain, factor, factor, factor],
        out_specs=pl.BlockSpec((8, 2, 32, 2 * BLOCK), lambda f: (0, f, 0, 0)),
        out_shape=pltpu.HBM((8, 2 * bins, 32, 2 * BLOCK), BF16),
        compiler_params=params(),
        cost_estimate=pl.CostEstimate(
            flops=bins * 2 * 2 * 768 * 256 * 512, bytes_accessed=bins * 5 << 18, transcendentals=0
        ),
        name="cross" + str(first),
    )(odd, s, n, u, fs, fn, fu)


def lag_sums(matrix_ref, cross_ref):
    cross = cross_ref[...].reshape(-1, 32, BLOCK)
    pair = jnp.concatenate([cross[:, :SUB], cross[:, SUB:]], axis=2)
    return lax.dot_general(
        matrix_ref[...],
        pair.reshape(cross.shape[0] * SUB, 2 * BLOCK),
        (((1,), (0,)), ((), ())),
        preferred_element_type=F32,
    )


def lags_kernel(scale, matrix_ref, cross_ref, out_ref):
    lagged = (lag_sums(matrix_ref, cross_ref) * scale).astype(BF16)
    for half in range(2):
        piece = lagged[:, half * BLOCK : (half + 1) * BLOCK].reshape(8, 4, SUB, BLOCK)
        out_ref[:, 0, :, half * SUB : (half + 1) * SUB] = piece


def to_lags(cross):
    return pl.pallas_call(
        functools.partial(lags_kernel, 1.0 / math.sqrt(FREQS * WIN)),
        grid=(2,),
        in_specs=[
            pl.BlockSpec((512, 2048), lambda c: (0, 0)),
            pl.BlockSpec((8, 16, 32, BLOCK), lambda c: (0, 0, 0, c)),
        ],
        out_specs=pl.BlockSpec((8, 1, 4, 32, BLOCK), lambda c: (0, c, 0, 0, 0)),
        out_shape=pltpu.HBM((8, 2, 4, 32, BLOCK), BF16),
        compiler_params=params(),
        cost_estimate=pl.CostEstimate(
            flops=2 * 512 * 2048 * 1024, bytes_accessed=7 << 20, transcendentals=0
        ),
        name="to_lags",
    )(lag_matrix(0, 8), cross)


def assemble_kernel(one_ref, two_ref, out_ref):
    for src in range(8):
        rows = slice(src * 32, src * 32 + 32)
        out_ref[0, :, rows] = one_ref[src]
        out_ref[1, :, rows] = two_ref[src]


def assemble(one, two):
    return pl.pallas_call(
        assemble_kernel,
        in_specs=[held_spec()] * 2,
        out_specs=held_spec(),
        out_shape=jax.ShapeDtypeStruct((2, 4, BLOCK, BLOCK), BF16),
        compiler_params=params(),
        cost_estimate=pl.CostEstimate(flops=0, bytes_accessed=2 << 20, transcendentals=0),
        name="assemble",
    )(one, two)


def exchange(value, partner):
    route = [(b, partner(b)) for b in range(8)]
    return lax.ppermute(value, "band", route)


def regroup(block):
    return lax.all_to_all(block, "band", split_axis=0, concat_axis=0, tiled=True)


def shards(spectra, window_valid):
    blocks = lax.axis_size("pair")
    flag = (lax.axis_index("pair") % 2).astype(jnp.int32).reshape(1)
    across = [((p + 2) % blocks, p) if p % 2 == 0 else ((p - 2) % blocks, p) for p in range(blocks)]
    swap = [(p ^ 1, p) for p in range(blocks)]
    back = [(p, p) if p % 2 == 0 else ((p + 2) % blocks, p) for p in range(blocks)]
    other = [((p + 3) % blocks, p) if p % 2 == 0 else ((p - 3) % blocks, p) for p in range(blocks)]
    barrier = lax.optimization_barrier

    values = spectra.astype(F32)
    energy = jnp.sum(values * values, axis=(0, 1))
    met, moved = barrier((exchange(energy.astype(BF16), lambda b: (b + 4) % 8), spectra))
    u = lax.ppermute(moved, "pair", across)
    energy = energy + met.astype(F32)
    energy = energy + exchange(energy.astype(BF16), lambda b: b ^ 1).astype(F32)
    energy, moved = barrier((energy, moved))
    n = lax.ppermute(moved, "pair", swap)
    energy = energy + exchange(energy.astype(BF16), lambda b: (b // 4) * 4 + 3 - b % 4).astype(F32)
    fs = (window_valid.astype(F32) * lax.rsqrt(energy / FREQS + EPSILON)).astype(BF16)
    fn = lax.ppermute(fs, "pair", swap)
    fu = lax.ppermute(fn, "pair", other)

    cross = cross_spectra(0, flag, spectra, n, u, fs, fn, fu)
    own = regroup(to_lags(regroup(cross)))
    return assemble(lax.ppermute(own[:, 0], "pair", swap), lax.ppermute(own[:, 1], "pair", back))


def solution(mesh):
    return jax.shard_map(
        shards,
        mesh=mesh,
        in_specs=(P("band", None, None, "pair"), P(None, "pair")),
        out_specs=P(None, "band", "pair", None),
        check_vma=False,
    )
```

```python
import functools
import math

import jax
import jax.numpy as jnp
import numpy as np
from jax import lax
from jax.experimental import pallas as pl
from jax.experimental.pallas import tpu as pltpu
from jax.sharding import PartitionSpec as P

FREQS = 64
KEEP = 32
WIN = 384
EPSILON = 1e-06
BLOCK = 256
SUB = 16
STEP = 2
VMEM_LIMIT = 28 * 1024 * 1024

BF16 = jnp.bfloat16
F32 = jnp.float32


def params():
    return pltpu.CompilerParams(vmem_limit_bytes=VMEM_LIMIT)


def lag_matrix(first, bins):
    lag_index = np.arange(KEEP, dtype=np.float32) - np.float32(KEEP // 2)
    bin_index = np.arange(FREQS, dtype=np.float32) + np.float32(1.0)
    step = np.float32(2.0 * math.pi / (2 * FREQS))
    phase = (step * lag_index)[:, None] * bin_index[None, :]
    table = np.stack([np.cos(phase), -np.sin(phase)], axis=2).reshape(KEEP, 8, 8, 2)
    table = table[:, :, first : first + bins].reshape(KEEP, 16 * bins)
    return jnp.asarray(np.kron(table, np.eye(SUB, dtype=np.float32)), dtype=BF16)


def whiten(raw, factor):
    if factor.dtype == BF16:
        return raw * factor[None]
    return (raw.astype(F32) * factor[None]).astype(BF16)


def product(left, right):
    windows = left.shape[1]
    rows = left.reshape(2 * windows, left.shape[2])
    top = jnp.concatenate([right[0], right[1]], axis=1)
    low = jnp.concatenate([right[1], -right[0]], axis=1)
    cols = jnp.concatenate([top, low], axis=0)
    return lax.dot_general(rows, cols, (((0,), (0,)), ((), ())), preferred_element_type=F32)


def store(out_ref, result):
    for part in range(2):
        piece = result[:, part * BLOCK : (part + 1) * BLOCK]
        out_ref[:, part] = piece.astype(BF16).reshape(8, 32, BLOCK)


def near_kernel(odd_ref, s_ref, n_ref, fs_ref, fn_ref, sw_ref, nw_ref, out_ref):
    for index in range(STEP):
        f = pl.program_id(0) * STEP + index
        sw_ref[f] = whiten(s_ref[f], fs_ref[...])
        nw_ref[f] = whiten(n_ref[index], fn_ref[...])

        @pl.when(odd_ref[0] != 0)
        def _():
            store(out_ref.at[:, 2 * index : 2 * index + 2], product(nw_ref[f], sw_ref[f]))


def far_kernel(first, odd_ref, own_ref, near_ref, u_ref, fu_ref, _, out_ref, held_ref, send_ref, in_sem, out_sem):
    bins = u_ref.shape[0]
    odd = odd_ref[0]

    def fetch(f):
        return pltpu.make_async_copy(u_ref.at[f], held_ref.at[f], in_sem.at[f])

    def put(f, part):
        rows, columns = pl.ds(2 * f, 2), pl.ds(part * BLOCK, BLOCK)
        return pltpu.make_async_copy(
            send_ref.at[:, rows, :, columns],
            out_ref.at[:, pl.ds(2 * (first + f), 2), :, columns],
            out_sem.at[part, f],
        )

    def made(f, part, left, right):
        store(send_ref.at[:, pl.ds(2 * f, 2), :, pl.ds(part * BLOCK, BLOCK)], product(left, right))
        put(f, part).start()

    for f in range(bins):
        fetch(f).start()

    def step(f, carry):
        fetch(f).wait()
        far = whiten(held_ref[f], fu_ref[...])
        own = own_ref[first + f]

        @pl.when(odd == 0)
        def _():
            made(f, 0, near_ref[first + f], far)
            made(f, 1, own, far)

        @pl.when(odd != 0)
        def _():
            made(f, 1, far, own)

        return carry

    lax.fori_loop(0, bins, step, 0)
    for f in range(bins):
        put(f, 1).wait()

    @pl.when(odd == 0)
    def _():
        for f in range(bins):
            put(f, 0).wait()


def flag_spec():
    return pl.BlockSpec(memory_space=pltpu.SMEM)


def held_spec():
    return pl.BlockSpec(memory_space=pltpu.VMEM)


SEND = (8, 16, 32, 2 * BLOCK)
SEND_BLOCK = (8, 2 * STEP, 32, BLOCK)
BINS_BLOCK = (STEP, 2, WIN, BLOCK)


def near_spectra(odd, s, n, fs, fn):
    shape = jax.ShapeDtypeStruct(s.shape, BF16)
    return pl.pallas_call(
        near_kernel,
        grid=(8 // STEP,),
        in_specs=[flag_spec(), held_spec(), pl.BlockSpec(BINS_BLOCK, lambda g: (g, 0, 0, 0)), held_spec(), held_spec()],
        out_specs=[held_spec(), held_spec(), pl.BlockSpec(SEND_BLOCK, lambda g: (0, g, 0, 0))],
        out_shape=[shape, shape, pltpu.HBM(SEND, BF16)],
        compiler_params=params(),
        cost_estimate=pl.CostEstimate(flops=0, bytes_accessed=0, transcendentals=0),
        name="near_spectra",
    )(odd, s, n, fs, fn)


def far_spectra(first, odd, own, near, u, fu, filled):
    bins = u.shape[0]
    anywhere = pl.BlockSpec(memory_space=pl.ANY)
    return pl.pallas_call(
        functools.partial(far_kernel, first),
        in_specs=[flag_spec(), held_spec(), held_spec(), anywhere, held_spec(), anywhere],
        out_specs=anywhere,
        out_shape=pltpu.HBM(SEND, BF16),
        scratch_shapes=[
            pltpu.VMEM((bins, 2, WIN, BLOCK), BF16),
            pltpu.VMEM((8, 2 * bins, 32, 2 * BLOCK), BF16),
            pltpu.SemaphoreType.DMA((bins,)),
            pltpu.SemaphoreType.DMA((2, bins)),
        ],
        input_output_aliases={5: 0},
        compiler_params=params(),
        cost_estimate=pl.CostEstimate(
            flops=bins * 2 * 2 * 768 * 256 * 512, bytes_accessed=bins << 20, transcendentals=0
        ),
        name="far" + str(first),
    )(odd, own, near, u, fu, filled)


def lags_kernel(scale, matrix_ref, cross_ref, out_ref):
    for part in range(2):
        columns = slice(part * BLOCK, (part + 1) * BLOCK)
        cross = cross_ref[:, :, :, columns].reshape(2 * FREQS, 32, BLOCK)
        pair = jnp.concatenate([cross[:, :SUB], cross[:, SUB:]], axis=2)
        lagged = lax.dot_general(
            matrix_ref[...],
            pair.reshape(2 * FREQS * SUB, 2 * BLOCK),
            (((1,), (0,)), ((), ())),
            preferred_element_type=F32,
        )
        lagged = (lagged * scale).astype(BF16)
        for half in range(2):
            piece = lagged[:, half * BLOCK : (half + 1) * BLOCK].reshape(8, 4, SUB, BLOCK)
            out_ref[:, part, :, half * SUB : (half + 1) * SUB] = piece


def to_lags(cross):
    return pl.pallas_call(
        functools.partial(lags_kernel, 1.0 / math.sqrt(FREQS * WIN)),
        in_specs=[held_spec()] * 2,
        out_specs=held_spec(),
        out_shape=jax.ShapeDtypeStruct((8, 2, 4, 32, BLOCK), BF16),
        compiler_params=params(),
        cost_estimate=pl.CostEstimate(
            flops=2 * 512 * 2048 * 1024, bytes_accessed=7 << 20, transcendentals=0
        ),
        name="to_lags",
    )(lag_matrix(0, 8), cross)


def assemble_kernel(one_ref, two_ref, out_ref):
    for src in range(8):
        rows = slice(src * 32, src * 32 + 32)
        out_ref[0, :, rows] = one_ref[src]
        out_ref[1, :, rows] = two_ref[src]


def assemble(one, two):
    return pl.pallas_call(
        assemble_kernel,
        in_specs=[held_spec()] * 2,
        out_specs=held_spec(),
        out_shape=jax.ShapeDtypeStruct((2, 4, BLOCK, BLOCK), BF16),
        compiler_params=params(),
        cost_estimate=pl.CostEstimate(flops=0, bytes_accessed=2 << 20, transcendentals=0),
        name="assemble",
    )(one, two)


def exchange(value, partner):
    route = [(b, partner(b)) for b in range(8)]
    return lax.ppermute(value, "band", route)


def regroup(block):
    return lax.all_to_all(block, "band", split_axis=0, concat_axis=0, tiled=True)


def shards(spectra, window_valid):
    blocks = lax.axis_size("pair")
    flag = (lax.axis_index("pair") % 2).astype(jnp.int32).reshape(1)
    across = [((p + 2) % blocks, p) if p % 2 == 0 else ((p - 2) % blocks, p) for p in range(blocks)]
    swap = [(p ^ 1, p) for p in range(blocks)]
    back = [(p, p) if p % 2 == 0 else ((p + 2) % blocks, p) for p in range(blocks)]
    other = [((p + 3) % blocks, p) if p % 2 == 0 else ((p - 3) % blocks, p) for p in range(blocks)]
    barrier = lax.optimization_barrier

    values = spectra.astype(F32)
    energy = jnp.sum(values * values, axis=(0, 1))
    met, whole = barrier((exchange(energy.astype(BF16), lambda b: (b + 4) % 8), spectra))
    n = lax.ppermute(whole, "pair", swap)
    u = lax.ppermute(whole, "pair", across)
    energy = energy + met.astype(F32)
    energy = energy + exchange(energy.astype(BF16), lambda b: b ^ 1).astype(F32)
    energy = energy + exchange(energy.astype(BF16), lambda b: (b // 4) * 4 + 3 - b % 4).astype(F32)
    fs = window_valid.astype(F32) * lax.rsqrt(energy / FREQS + EPSILON)
    fn = lax.ppermute(fs.astype(BF16), "pair", swap)
    fu = lax.ppermute(fn, "pair", other)

    sw, nw, cross = near_spectra(flag, spectra, n, fs, fn)
    cross = far_spectra(0, flag, sw, nw, u, fu, cross)
    own = regroup(to_lags(regroup(cross)))
    return assemble(lax.ppermute(own[:, 0], "pair", swap), lax.ppermute(own[:, 1], "pair", back))


def solution(mesh):
    return jax.shard_map(
        shards,
        mesh=mesh,
        in_specs=(P("band", None, None, "pair"), P(None, "pair")),
        out_specs=P(None, "band", "pair", None),
        check_vma=False,
    )
```

```python
import functools
import math

import jax
import jax.numpy as jnp
import numpy as np
from jax import lax
from jax.experimental import pallas as pl
from jax.experimental.pallas import tpu as pltpu
from jax.sharding import PartitionSpec as P

FREQS = 64
KEEP = 32
WIN = 384
EPSILON = 1e-06
BLOCK = 256
SUB = 16
STEP = 2
CUTS = (0, 6, 8)
VMEM_LIMIT = 28 * 1024 * 1024

BF16 = jnp.bfloat16
F32 = jnp.float32


def params():
    return pltpu.CompilerParams(vmem_limit_bytes=VMEM_LIMIT)


def lag_matrix(first, bins):
    lag_index = np.arange(KEEP, dtype=np.float32) - np.float32(KEEP // 2)
    bin_index = np.arange(FREQS, dtype=np.float32) + np.float32(1.0)
    step = np.float32(2.0 * math.pi / (2 * FREQS))
    phase = (step * lag_index)[:, None] * bin_index[None, :]
    table = np.stack([np.cos(phase), -np.sin(phase)], axis=2).reshape(KEEP, 8, 8, 2)
    table = table[:, :, first : first + bins].reshape(KEEP, 16 * bins)
    return jnp.asarray(np.kron(table, np.eye(SUB, dtype=np.float32)), dtype=BF16)


def whiten(raw, factor):
    if factor.dtype == BF16:
        return raw * factor[None]
    return (raw.astype(F32) * factor[None]).astype(BF16)


def product(left, right):
    windows = left.shape[1]
    rows = left.reshape(2 * windows, left.shape[2])
    top = jnp.concatenate([right[0], right[1]], axis=1)
    low = jnp.concatenate([right[1], -right[0]], axis=1)
    cols = jnp.concatenate([top, low], axis=0)
    return lax.dot_general(rows, cols, (((0,), (0,)), ((), ())), preferred_element_type=F32)


def store(out_ref, result):
    for part in range(2):
        piece = result[:, part * BLOCK : (part + 1) * BLOCK]
        out_ref[:, part] = piece.astype(BF16).reshape(8, 32, BLOCK)


def near_kernel(starts, odd_ref, s_ref, fs_ref, fn_ref, *refs):
    pieces, (sw_ref, nw_ref, out_ref) = refs[:-3], refs[-3:]
    step = pl.program_id(0)
    for index in range(STEP):
        f = step * STEP + index
        for n_ref, first, last in zip(pieces, starts, starts[1:]):

            @pl.when((step >= first // STEP) & (step < last // STEP))
            def _():
                nw_ref[f] = n_ref[index]

        @pl.when(odd_ref[0] == 0)
        def _():
            sw_ref[f] = s_ref[f]

        @pl.when(odd_ref[0] != 0)
        def _():
            sw_ref[f] = whiten(s_ref[f], fs_ref[...])
            nw_ref[f] = whiten(nw_ref[f], fn_ref[...])
            store(out_ref.at[:, 2 * index : 2 * index + 2], product(nw_ref[f], sw_ref[f]))


def far_kernel(first, odd_ref, own_ref, near_ref, u_ref, fs_ref, fn_ref, fu_ref, _, out_ref, held_ref, send_ref, in_sem, out_sem):
    bins = u_ref.shape[0]
    odd = odd_ref[0]

    def fetch(f):
        return pltpu.make_async_copy(u_ref.at[f], held_ref.at[f], in_sem.at[f])

    def put(f, part):
        rows, columns = pl.ds(2 * f, 2), pl.ds(part * BLOCK, BLOCK)
        return pltpu.make_async_copy(
            send_ref.at[:, rows, :, columns],
            out_ref.at[:, pl.ds(2 * (first + f), 2), :, columns],
            out_sem.at[part, f],
        )

    def made(f, part, left, right):
        store(send_ref.at[:, pl.ds(2 * f, 2), :, pl.ds(part * BLOCK, BLOCK)], product(left, right))
        put(f, part).start()

    for f in range(bins):
        fetch(f).start()

    def step(f, carry):
        fetch(f).wait()
        far = whiten(held_ref[f], fu_ref[...])

        @pl.when(odd == 0)
        def _():
            made(f, 0, whiten(near_ref[first + f], fn_ref[...]), far)
            made(f, 1, whiten(own_ref[first + f], fs_ref[...]), far)

        @pl.when(odd != 0)
        def _():
            made(f, 1, far, own_ref[first + f])

        return carry

    lax.fori_loop(0, bins, step, 0)
    for f in range(bins):
        put(f, 1).wait()

    @pl.when(odd == 0)
    def _():
        for f in range(bins):
            put(f, 0).wait()


def flag_spec():
    return pl.BlockSpec(memory_space=pltpu.SMEM)


def held_spec():
    return pl.BlockSpec(memory_space=pltpu.VMEM)


SEND = (8, 16, 32, 2 * BLOCK)
SEND_BLOCK = (8, 2 * STEP, 32, BLOCK)
BINS_BLOCK = (STEP, 2, WIN, BLOCK)


def near_spectra(odd, s, fs, fn, pieces):
    shape = jax.ShapeDtypeStruct(s.shape, BF16)
    starts = [0]
    for piece in pieces:
        starts.append(starts[-1] + piece.shape[0])

    def piece_spec(first, last):
        return pl.BlockSpec(
            BINS_BLOCK, lambda g: (jnp.clip(g - first // STEP, 0, (last - first) // STEP - 1), 0, 0, 0)
        )

    return pl.pallas_call(
        functools.partial(near_kernel, starts),
        grid=(8 // STEP,),
        in_specs=[flag_spec(), held_spec(), held_spec(), held_spec()]
        + [piece_spec(first, last) for first, last in zip(starts, starts[1:])],
        out_specs=[held_spec(), held_spec(), pl.BlockSpec(SEND_BLOCK, lambda g: (0, g, 0, 0))],
        out_shape=[shape, shape, pltpu.HBM(SEND, BF16)],
        compiler_params=params(),
        cost_estimate=pl.CostEstimate(flops=0, bytes_accessed=0, transcendentals=0),
        name="near_spectra",
    )(odd, s, fs, fn, *pieces)


def far_spectra(first, odd, own, near, u, fs, fn, fu, filled):
    bins = u.shape[0]
    anywhere = pl.BlockSpec(memory_space=pl.ANY)
    return pl.pallas_call(
        functools.partial(far_kernel, first),
        in_specs=[flag_spec(), held_spec(), held_spec(), anywhere] + [held_spec()] * 3 + [anywhere],
        out_specs=anywhere,
        out_shape=pltpu.HBM(SEND, BF16),
        scratch_shapes=[
            pltpu.VMEM((bins, 2, WIN, BLOCK), BF16),
            pltpu.VMEM((8, 2 * bins, 32, 2 * BLOCK), BF16),
            pltpu.SemaphoreType.DMA((bins,)),
            pltpu.SemaphoreType.DMA((2, bins)),
        ],
        input_output_aliases={7: 0},
        compiler_params=params(),
        cost_estimate=pl.CostEstimate(
            flops=bins * 2 * 2 * 768 * 256 * 512, bytes_accessed=bins << 20, transcendentals=0
        ),
        name="far" + str(first),
    )(odd, own, near, u, fs, fn, fu, filled)


def lags_kernel(scale, matrix_ref, cross_ref, out_ref):
    for part in range(2):
        columns = slice(part * BLOCK, (part + 1) * BLOCK)
        cross = cross_ref[:, :, :, columns].reshape(2 * FREQS, 32, BLOCK)
        pair = jnp.concatenate([cross[:, :SUB], cross[:, SUB:]], axis=2)
        lagged = lax.dot_general(
            matrix_ref[...],
            pair.reshape(2 * FREQS * SUB, 2 * BLOCK),
            (((1,), (0,)), ((), ())),
            preferred_element_type=F32,
        )
        lagged = (lagged * scale).astype(BF16)
        for half in range(2):
            piece = lagged[:, half * BLOCK : (half + 1) * BLOCK].reshape(8, 4, SUB, BLOCK)
            out_ref[:, part, :, half * SUB : (half + 1) * SUB] = piece


def to_lags(cross):
    return pl.pallas_call(
        functools.partial(lags_kernel, 1.0 / math.sqrt(FREQS * WIN)),
        in_specs=[held_spec()] * 2,
        out_specs=held_spec(),
        out_shape=jax.ShapeDtypeStruct((8, 2, 4, 32, BLOCK), BF16),
        compiler_params=params(),
        cost_estimate=pl.CostEstimate(
            flops=2 * 512 * 2048 * 1024, bytes_accessed=7 << 20, transcendentals=0
        ),
        name="to_lags",
    )(lag_matrix(0, 8), cross)


def assemble_kernel(one_ref, two_ref, out_ref):
    for src in range(8):
        rows = slice(src * 32, src * 32 + 32)
        out_ref[0, :, rows] = one_ref[src]
        out_ref[1, :, rows] = two_ref[src]


def assemble(one, two):
    return pl.pallas_call(
        assemble_kernel,
        in_specs=[held_spec()] * 2,
        out_specs=held_spec(),
        out_shape=jax.ShapeDtypeStruct((2, 4, BLOCK, BLOCK), BF16),
        compiler_params=params(),
        cost_estimate=pl.CostEstimate(flops=0, bytes_accessed=2 << 20, transcendentals=0),
        name="assemble",
    )(one, two)


def exchange(value, partner):
    route = [(b, partner(b)) for b in range(8)]
    return lax.ppermute(value, "band", route)


def regroup(block):
    return lax.all_to_all(block, "band", split_axis=0, concat_axis=0, tiled=True)


def shards(spectra, window_valid):
    blocks = lax.axis_size("pair")
    flag = (lax.axis_index("pair") % 2).astype(jnp.int32).reshape(1)
    across = [((p + 2) % blocks, p) if p % 2 == 0 else ((p - 2) % blocks, p) for p in range(blocks)]
    swap = [(p ^ 1, p) for p in range(blocks)]
    back = [(p, p) if p % 2 == 0 else ((p + 2) % blocks, p) for p in range(blocks)]
    barrier = lax.optimization_barrier

    values = spectra.astype(F32)
    energy = jnp.sum(values * values, axis=(0, 1))
    pieces = [spectra[first:last] for first, last in zip(CUTS, CUTS[1:])]
    met, whole, pieces = barrier((exchange(energy.astype(BF16), lambda b: (b + 4) % 8), spectra, pieces))
    u = lax.ppermute(whole, "pair", across)
    pieces = [lax.ppermute(piece, "pair", swap) for piece in pieces]
    energy = energy + met.astype(F32)
    energy = energy + exchange(energy.astype(BF16), lambda b: b ^ 1).astype(F32)
    energy = energy + exchange(energy.astype(BF16), lambda b: (b // 4) * 4 + 3 - b % 4).astype(F32)
    fs = window_valid.astype(F32) * lax.rsqrt(energy / FREQS + EPSILON)
    fn = lax.ppermute(fs.astype(BF16), "pair", swap)
    fu = lax.ppermute(fs.astype(BF16), "pair", across)

    sw, nw, cross = near_spectra(flag, spectra, fs, fn, pieces)
    cross = far_spectra(0, flag, sw, nw, u, fs, fn, fu, cross)
    own = regroup(to_lags(regroup(cross)))
    return assemble(lax.ppermute(own[:, 0], "pair", swap), lax.ppermute(own[:, 1], "pair", back))


def solution(mesh):
    return jax.shard_map(
        shards,
        mesh=mesh,
        in_specs=(P("band", None, None, "pair"), P(None, "pair")),
        out_specs=P(None, "band", "pair", None),
        check_vma=False,
    )
```

```python
import functools
import math

import jax
import jax.numpy as jnp
import numpy as np
from jax import lax
from jax.experimental import pallas as pl
from jax.experimental.pallas import tpu as pltpu
from jax.sharding import PartitionSpec as P

FREQS = 64
KEEP = 32
WIN = 384
EPSILON = 1e-06
BLOCK = 256
SUB = 16
STEP = 2
CUTS = (0, 6, 8)
VMEM_LIMIT = 28 * 1024 * 1024

BF16 = jnp.bfloat16
F32 = jnp.float32


def params():
    return pltpu.CompilerParams(vmem_limit_bytes=VMEM_LIMIT)


def lag_matrix(first, bins):
    lag_index = np.arange(KEEP, dtype=np.float32) - np.float32(KEEP // 2)
    bin_index = np.arange(FREQS, dtype=np.float32) + np.float32(1.0)
    step = np.float32(2.0 * math.pi / (2 * FREQS))
    phase = (step * lag_index)[:, None] * bin_index[None, :]
    table = np.stack([np.cos(phase), -np.sin(phase)], axis=2).reshape(KEEP, 8, 8, 2)
    table = table[:, :, first : first + bins].reshape(KEEP, 16 * bins)
    return jnp.asarray(np.kron(table, np.eye(SUB, dtype=np.float32)), dtype=BF16)


def whiten(raw, factor):
    if factor.dtype == BF16:
        return raw * factor[None]
    return (raw.astype(F32) * factor[None]).astype(BF16)


def product(left, right):
    windows = left.shape[1]
    rows = left.reshape(2 * windows, left.shape[2])
    top = jnp.concatenate([right[0], right[1]], axis=1)
    low = jnp.concatenate([right[1], -right[0]], axis=1)
    cols = jnp.concatenate([top, low], axis=0)
    return lax.dot_general(rows, cols, (((0,), (0,)), ((), ())), preferred_element_type=F32)


def store(out_ref, result):
    for part in range(2):
        piece = result[:, part * BLOCK : (part + 1) * BLOCK]
        out_ref[:, part] = piece.astype(BF16).reshape(8, 32, BLOCK)


def near_kernel(starts, odd_ref, s_ref, fs_ref, fn_ref, *refs):
    pieces, (sw_ref, nw_ref, out_ref) = refs[:-3], refs[-3:]
    step = pl.program_id(0)
    for index in range(STEP):
        f = step * STEP + index
        for n_ref, first, last in zip(pieces, starts, starts[1:]):

            @pl.when((step >= first // STEP) & (step < last // STEP))
            def _():
                nw_ref[f] = n_ref[index]

        @pl.when(odd_ref[0] == 0)
        def _():
            sw_ref[f] = s_ref[f]

        @pl.when(odd_ref[0] != 0)
        def _():
            sw_ref[f] = whiten(s_ref[f], fs_ref[...])
            nw_ref[f] = whiten(nw_ref[f], fn_ref[...])
            store(out_ref.at[:, 2 * index : 2 * index + 2], product(nw_ref[f], sw_ref[f]))


def far_kernel(first, odd_ref, own_ref, near_ref, u_ref, fs_any, fn_any, fu_any, _, out_ref, held_ref, fs_ref, fn_ref, fu_ref, send_ref, in_sem, factor_sem, out_sem):
    bins = u_ref.shape[0]
    odd = odd_ref[0]

    def fetch(f):
        return pltpu.make_async_copy(u_ref.at[f], held_ref.at[f], in_sem.at[f])

    def put(f, part):
        rows, columns = pl.ds(2 * f, 2), pl.ds(part * BLOCK, BLOCK)
        return pltpu.make_async_copy(
            send_ref.at[:, rows, :, columns],
            out_ref.at[:, pl.ds(2 * (first + f), 2), :, columns],
            out_sem.at[part, f],
        )

    def made(f, part, left, right):
        store(send_ref.at[:, pl.ds(2 * f, 2), :, pl.ds(part * BLOCK, BLOCK)], product(left, right))
        put(f, part).start()

    def factor(index):
        pairs = ((fu_any, fu_ref), (fs_any, fs_ref), (fn_any, fn_ref))
        return pltpu.make_async_copy(*pairs[index], factor_sem.at[index])

    factor(0).start()
    fetch(0).start()

    @pl.when(odd == 0)
    def _():
        factor(1).start()
        factor(2).start()

    for f in range(1, bins):
        fetch(f).start()
    factor(0).wait()

    @pl.when(odd == 0)
    def _():
        factor(1).wait()
        factor(2).wait()

    def step(f, carry):
        fetch(f).wait()
        far = whiten(held_ref[f], fu_ref[...])

        @pl.when(odd == 0)
        def _():
            made(f, 0, whiten(near_ref[first + f], fn_ref[...]), far)
            made(f, 1, whiten(own_ref[first + f], fs_ref[...]), far)

        @pl.when(odd != 0)
        def _():
            made(f, 1, far, own_ref[first + f])

        return carry

    lax.fori_loop(0, bins, step, 0)
    for f in range(bins):
        put(f, 1).wait()

    @pl.when(odd == 0)
    def _():
        for f in range(bins):
            put(f, 0).wait()


def flag_spec():
    return pl.BlockSpec(memory_space=pltpu.SMEM)


def held_spec():
    return pl.BlockSpec(memory_space=pltpu.VMEM)


SEND = (8, 16, 32, 2 * BLOCK)
SEND_BLOCK = (8, 2 * STEP, 32, BLOCK)
BINS_BLOCK = (STEP, 2, WIN, BLOCK)


def near_spectra(odd, s, fs, fn, pieces):
    shape = jax.ShapeDtypeStruct(s.shape, BF16)
    starts = [0]
    for piece in pieces:
        starts.append(starts[-1] + piece.shape[0])

    def piece_spec(first, last):
        return pl.BlockSpec(
            BINS_BLOCK, lambda g: (jnp.clip(g - first // STEP, 0, (last - first) // STEP - 1), 0, 0, 0)
        )

    return pl.pallas_call(
        functools.partial(near_kernel, starts),
        grid=(8 // STEP,),
        in_specs=[flag_spec(), held_spec(), held_spec(), held_spec()]
        + [piece_spec(first, last) for first, last in zip(starts, starts[1:])],
        out_specs=[held_spec(), held_spec(), pl.BlockSpec(SEND_BLOCK, lambda g: (0, g, 0, 0))],
        out_shape=[shape, shape, pltpu.HBM(SEND, BF16)],
        compiler_params=params(),
        cost_estimate=pl.CostEstimate(flops=0, bytes_accessed=0, transcendentals=0),
        name="near_spectra",
    )(odd, s, fs, fn, *pieces)


def far_spectra(first, odd, own, near, u, fs, fn, fu, filled):
    bins = u.shape[0]
    anywhere = pl.BlockSpec(memory_space=pl.ANY)
    return pl.pallas_call(
        functools.partial(far_kernel, first),
        in_specs=[flag_spec(), held_spec(), held_spec()] + [anywhere] * 5,
        out_specs=anywhere,
        out_shape=pltpu.HBM(SEND, BF16),
        scratch_shapes=[
            pltpu.VMEM((bins, 2, WIN, BLOCK), BF16),
            pltpu.VMEM((WIN, BLOCK), fs.dtype),
            pltpu.VMEM((WIN, BLOCK), fn.dtype),
            pltpu.VMEM((WIN, BLOCK), fu.dtype),
            pltpu.VMEM((8, 2 * bins, 32, 2 * BLOCK), BF16),
            pltpu.SemaphoreType.DMA((bins,)),
            pltpu.SemaphoreType.DMA((3,)),
            pltpu.SemaphoreType.DMA((2, bins)),
        ],
        input_output_aliases={7: 0},
        compiler_params=params(),
        cost_estimate=pl.CostEstimate(
            flops=bins * 2 * 2 * 768 * 256 * 512, bytes_accessed=bins << 20, transcendentals=0
        ),
        name="far" + str(first),
    )(odd, own, near, u, fs, fn, fu, filled)


def lags_kernel(scale, matrix_ref, cross_ref, out_ref):
    for part in range(2):
        columns = slice(part * BLOCK, (part + 1) * BLOCK)
        cross = cross_ref[:, :, :, columns].reshape(2 * FREQS, 32, BLOCK)
        pair = jnp.concatenate([cross[:, :SUB], cross[:, SUB:]], axis=2)
        lagged = lax.dot_general(
            matrix_ref[...],
            pair.reshape(2 * FREQS * SUB, 2 * BLOCK),
            (((1,), (0,)), ((), ())),
            preferred_element_type=F32,
        )
        lagged = (lagged * scale).astype(BF16)
        for half in range(2):
            piece = lagged[:, half * BLOCK : (half + 1) * BLOCK].reshape(8, 4, SUB, BLOCK)
            out_ref[:, part, :, half * SUB : (half + 1) * SUB] = piece


def to_lags(cross):
    return pl.pallas_call(
        functools.partial(lags_kernel, 1.0 / math.sqrt(FREQS * WIN)),
        in_specs=[held_spec()] * 2,
        out_specs=held_spec(),
        out_shape=jax.ShapeDtypeStruct((8, 2, 4, 32, BLOCK), BF16),
        compiler_params=params(),
        cost_estimate=pl.CostEstimate(
            flops=2 * 512 * 2048 * 1024, bytes_accessed=7 << 20, transcendentals=0
        ),
        name="to_lags",
    )(lag_matrix(0, 8), cross)


def assemble_kernel(one_ref, two_ref, out_ref):
    for src in range(8):
        rows = slice(src * 32, src * 32 + 32)
        out_ref[0, :, rows] = one_ref[src]
        out_ref[1, :, rows] = two_ref[src]


def assemble(one, two):
    return pl.pallas_call(
        assemble_kernel,
        in_specs=[held_spec()] * 2,
        out_specs=held_spec(),
        out_shape=jax.ShapeDtypeStruct((2, 4, BLOCK, BLOCK), BF16),
        compiler_params=params(),
        cost_estimate=pl.CostEstimate(flops=0, bytes_accessed=2 << 20, transcendentals=0),
        name="assemble",
    )(one, two)


def exchange(value, partner):
    route = [(b, partner(b)) for b in range(8)]
    return lax.ppermute(value, "band", route)


def regroup(block):
    return lax.all_to_all(block, "band", split_axis=0, concat_axis=0, tiled=True)


def shards(spectra, window_valid):
    blocks = lax.axis_size("pair")
    flag = (lax.axis_index("pair") % 2).astype(jnp.int32).reshape(1)
    across = [((p + 2) % blocks, p) if p % 2 == 0 else ((p - 2) % blocks, p) for p in range(blocks)]
    swap = [(p ^ 1, p) for p in range(blocks)]
    back = [(p, p) if p % 2 == 0 else ((p + 2) % blocks, p) for p in range(blocks)]
    barrier = lax.optimization_barrier

    values = spectra.astype(F32)
    energy = jnp.sum(values * values, axis=(0, 1))
    pieces = [spectra[first:last] for first, last in zip(CUTS, CUTS[1:])]
    met, whole, pieces = barrier((exchange(energy.astype(BF16), lambda b: (b + 4) % 8), spectra, pieces))
    u = lax.ppermute(whole, "pair", across)
    pieces = [lax.ppermute(piece, "pair", swap) for piece in pieces]
    energy = energy + met.astype(F32)
    energy = energy + exchange(energy.astype(BF16), lambda b: b ^ 1).astype(F32)
    energy = energy + exchange(energy.astype(BF16), lambda b: (b // 4) * 4 + 3 - b % 4).astype(F32)
    fs = window_valid.astype(F32) * lax.rsqrt(energy / FREQS + EPSILON)
    fn = lax.ppermute(fs.astype(BF16), "pair", swap)
    fu = lax.ppermute(fs.astype(BF16), "pair", across)

    sw, nw, cross = near_spectra(flag, spectra, fs, fn, pieces)
    cross = far_spectra(0, flag, sw, nw, u, fs, fn, fu, cross)
    own = regroup(to_lags(regroup(cross)))
    return assemble(lax.ppermute(own[:, 0], "pair", swap), lax.ppermute(own[:, 1], "pair", back))


def solution(mesh):
    return jax.shard_map(
        shards,
        mesh=mesh,
        in_specs=(P("band", None, None, "pair"), P(None, "pair")),
        out_specs=P(None, "band", "pair", None),
        check_vma=False,
    )
```

```python
import functools
import math

import jax
import jax.numpy as jnp
import numpy as np
from jax import lax
from jax.experimental import pallas as pl
from jax.experimental.pallas import tpu as pltpu
from jax.sharding import PartitionSpec as P

FREQS = 64
KEEP = 32
WIN = 384
EPSILON = 1e-06
BLOCK = 256
SUB = 16
STEP = 2
CUTS = (0, 6, 8)
VMEM_LIMIT = 28 * 1024 * 1024

BF16 = jnp.bfloat16
F32 = jnp.float32


def params():
    return pltpu.CompilerParams(vmem_limit_bytes=VMEM_LIMIT)


def lag_matrix(first, bins):
    lag_index = np.arange(KEEP, dtype=np.float32) - np.float32(KEEP // 2)
    bin_index = np.arange(FREQS, dtype=np.float32) + np.float32(1.0)
    step = np.float32(2.0 * math.pi / (2 * FREQS))
    phase = (step * lag_index)[:, None] * bin_index[None, :]
    table = np.stack([np.cos(phase), -np.sin(phase)], axis=2).reshape(KEEP, 8, 8, 2)
    table = table[:, :, first : first + bins].reshape(KEEP, 16 * bins)
    return jnp.asarray(np.kron(table, np.eye(SUB, dtype=np.float32)), dtype=BF16)


def whiten(raw, factor):
    if factor.dtype == BF16:
        return raw * factor[None]
    return (raw.astype(F32) * factor[None]).astype(BF16)


def product(left, right):
    windows = left.shape[1]
    rows = left.reshape(2 * windows, left.shape[2])
    top = jnp.concatenate([right[0], right[1]], axis=1)
    low = jnp.concatenate([right[1], -right[0]], axis=1)
    cols = jnp.concatenate([top, low], axis=0)
    return lax.dot_general(rows, cols, (((0,), (0,)), ((), ())), preferred_element_type=F32)


def store(out_ref, result):
    for part in range(2):
        piece = result[:, part * BLOCK : (part + 1) * BLOCK]
        out_ref[:, part] = piece.astype(BF16).reshape(8, 32, BLOCK)


def near_kernel(starts, odd_ref, s_ref, fs_ref, fn_ref, *refs):
    pieces, (sw_ref, nw_ref, out_ref) = refs[:-3], refs[-3:]
    step = pl.program_id(0)
    for index in range(STEP):
        f = step * STEP + index
        for n_ref, first, last in zip(pieces, starts, starts[1:]):

            @pl.when((step >= first // STEP) & (step < last // STEP))
            def _():
                nw_ref[f] = n_ref[index]

        sw_ref[f] = whiten(s_ref[f], fs_ref[...])

        @pl.when(odd_ref[0] != 0)
        def _():
            nw_ref[f] = whiten(nw_ref[f], fn_ref[...])
            store(out_ref.at[:, 2 * index : 2 * index + 2], product(nw_ref[f], sw_ref[f]))


def far_kernel(first, odd_ref, own_ref, near_ref, u_ref, fs_any, fn_any, fu_any, _, out_ref, held_ref, fs_ref, fn_ref, fu_ref, send_ref, in_sem, factor_sem, out_sem):
    bins = u_ref.shape[0]
    odd = odd_ref[0]

    def fetch(f):
        return pltpu.make_async_copy(u_ref.at[f], held_ref.at[f], in_sem.at[f])

    def put(f, part):
        rows, columns = pl.ds(2 * f, 2), pl.ds(part * BLOCK, BLOCK)
        return pltpu.make_async_copy(
            send_ref.at[:, rows, :, columns],
            out_ref.at[:, pl.ds(2 * (first + f), 2), :, columns],
            out_sem.at[part, f],
        )

    def made(f, part, left, right):
        store(send_ref.at[:, pl.ds(2 * f, 2), :, pl.ds(part * BLOCK, BLOCK)], product(left, right))
        put(f, part).start()

    def factor(index):
        pairs = ((fu_any, fu_ref), (fs_any, fs_ref), (fn_any, fn_ref))
        return pltpu.make_async_copy(*pairs[index], factor_sem.at[index])

    factor(0).start()
    fetch(0).start()

    @pl.when(odd == 0)
    def _():
        factor(1).start()
        factor(2).start()

    for f in range(1, bins):
        fetch(f).start()
    factor(0).wait()

    @pl.when(odd == 0)
    def _():
        factor(1).wait()
        factor(2).wait()

    def step(f, carry):
        fetch(f).wait()
        far = whiten(held_ref[f], fu_ref[...])

        @pl.when(odd == 0)
        def _():
            made(f, 0, whiten(near_ref[first + f], fn_ref[...]), far)
            made(f, 1, own_ref[first + f], far)

        @pl.when(odd != 0)
        def _():
            made(f, 1, far, own_ref[first + f])

        return carry

    lax.fori_loop(0, bins, step, 0, unroll=2)
    for f in range(bins):
        put(f, 1).wait()

    @pl.when(odd == 0)
    def _():
        for f in range(bins):
            put(f, 0).wait()


def flag_spec():
    return pl.BlockSpec(memory_space=pltpu.SMEM)


def held_spec():
    return pl.BlockSpec(memory_space=pltpu.VMEM)


SEND = (8, 16, 32, 2 * BLOCK)
SEND_BLOCK = (8, 2 * STEP, 32, BLOCK)
BINS_BLOCK = (STEP, 2, WIN, BLOCK)


def near_spectra(odd, s, fs, fn, pieces):
    shape = jax.ShapeDtypeStruct(s.shape, BF16)
    starts = [0]
    for piece in pieces:
        starts.append(starts[-1] + piece.shape[0])

    def piece_spec(first, last):
        return pl.BlockSpec(
            BINS_BLOCK, lambda g: (jnp.clip(g - first // STEP, 0, (last - first) // STEP - 1), 0, 0, 0)
        )

    return pl.pallas_call(
        functools.partial(near_kernel, starts),
        grid=(8 // STEP,),
        in_specs=[flag_spec(), held_spec(), held_spec(), held_spec()]
        + [piece_spec(first, last) for first, last in zip(starts, starts[1:])],
        out_specs=[held_spec(), held_spec(), pl.BlockSpec(SEND_BLOCK, lambda g: (0, g, 0, 0))],
        out_shape=[shape, shape, pltpu.HBM(SEND, BF16)],
        compiler_params=params(),
        cost_estimate=pl.CostEstimate(flops=0, bytes_accessed=0, transcendentals=0),
        name="near_spectra",
    )(odd, s, fs, fn, *pieces)


def far_spectra(first, odd, own, near, u, fs, fn, fu, filled):
    bins = u.shape[0]
    anywhere = pl.BlockSpec(memory_space=pl.ANY)
    return pl.pallas_call(
        functools.partial(far_kernel, first),
        in_specs=[flag_spec(), held_spec(), held_spec()] + [anywhere] * 5,
        out_specs=anywhere,
        out_shape=pltpu.HBM(SEND, BF16),
        scratch_shapes=[
            pltpu.VMEM((bins, 2, WIN, BLOCK), BF16),
            pltpu.VMEM((WIN, BLOCK), fs.dtype),
            pltpu.VMEM((WIN, BLOCK), fn.dtype),
            pltpu.VMEM((WIN, BLOCK), fu.dtype),
            pltpu.VMEM((8, 2 * bins, 32, 2 * BLOCK), BF16),
            pltpu.SemaphoreType.DMA((bins,)),
            pltpu.SemaphoreType.DMA((3,)),
            pltpu.SemaphoreType.DMA((2, bins)),
        ],
        input_output_aliases={7: 0},
        compiler_params=params(),
        cost_estimate=pl.CostEstimate(
            flops=bins * 2 * 2 * 768 * 256 * 512, bytes_accessed=bins << 20, transcendentals=0
        ),
        name="far" + str(first),
    )(odd, own, near, u, fs, fn, fu, filled)


def lags_kernel(scale, matrix_ref, cross_ref, out_ref):
    for part in range(2):
        columns = slice(part * BLOCK, (part + 1) * BLOCK)
        cross = cross_ref[:, :, :, columns].reshape(2 * FREQS, 32, BLOCK)
        pair = jnp.concatenate([cross[:, :SUB], cross[:, SUB:]], axis=2)
        lagged = lax.dot_general(
            matrix_ref[...],
            pair.reshape(2 * FREQS * SUB, 2 * BLOCK),
            (((1,), (0,)), ((), ())),
            preferred_element_type=F32,
        )
        lagged = (lagged * scale).astype(BF16)
        for half in range(2):
            piece = lagged[:, half * BLOCK : (half + 1) * BLOCK].reshape(8, 4, SUB, BLOCK)
            out_ref[:, part, :, half * SUB : (half + 1) * SUB] = piece


def to_lags(cross):
    return pl.pallas_call(
        functools.partial(lags_kernel, 1.0 / math.sqrt(FREQS * WIN)),
        in_specs=[held_spec()] * 2,
        out_specs=held_spec(),
        out_shape=jax.ShapeDtypeStruct((8, 2, 4, 32, BLOCK), BF16),
        compiler_params=params(),
        cost_estimate=pl.CostEstimate(
            flops=2 * 512 * 2048 * 1024, bytes_accessed=7 << 20, transcendentals=0
        ),
        name="to_lags",
    )(lag_matrix(0, 8), cross)


def assemble_kernel(one_ref, two_ref, out_ref):
    for src in range(8):
        rows = slice(src * 32, src * 32 + 32)
        out_ref[0, :, rows] = one_ref[src]
        out_ref[1, :, rows] = two_ref[src]


def assemble(one, two):
    return pl.pallas_call(
        assemble_kernel,
        in_specs=[held_spec()] * 2,
        out_specs=held_spec(),
        out_shape=jax.ShapeDtypeStruct((2, 4, BLOCK, BLOCK), BF16),
        compiler_params=params(),
        cost_estimate=pl.CostEstimate(flops=0, bytes_accessed=2 << 20, transcendentals=0),
        name="assemble",
    )(one, two)


def exchange(value, partner):
    route = [(b, partner(b)) for b in range(8)]
    return lax.ppermute(value, "band", route)


def regroup(block):
    return lax.all_to_all(block, "band", split_axis=0, concat_axis=0, tiled=True)


def shards(spectra, window_valid):
    blocks = lax.axis_size("pair")
    flag = (lax.axis_index("pair") % 2).astype(jnp.int32).reshape(1)
    across = [((p + 2) % blocks, p) if p % 2 == 0 else ((p - 2) % blocks, p) for p in range(blocks)]
    swap = [(p ^ 1, p) for p in range(blocks)]
    back = [(p, p) if p % 2 == 0 else ((p + 2) % blocks, p) for p in range(blocks)]
    barrier = lax.optimization_barrier

    values = spectra.astype(F32)
    energy = jnp.sum(values * values, axis=(0, 1))
    pieces = [spectra[first:last] for first, last in zip(CUTS, CUTS[1:])]
    met, whole, pieces = barrier((exchange(energy.astype(BF16), lambda b: (b + 4) % 8), spectra, pieces))
    u = lax.ppermute(whole, "pair", across)
    pieces = [lax.ppermute(piece, "pair", swap) for piece in pieces]
    energy = energy + met.astype(F32)
    energy = energy + exchange(energy.astype(BF16), lambda b: b ^ 1).astype(F32)
    energy = energy + exchange(energy.astype(BF16), lambda b: (b // 4) * 4 + 3 - b % 4).astype(F32)
    fs = window_valid.astype(F32) * lax.rsqrt(energy / FREQS + EPSILON)
    fn = lax.ppermute(fs.astype(BF16), "pair", swap)
    fu = lax.ppermute(fs.astype(BF16), "pair", across)

    sw, nw, cross = near_spectra(flag, spectra, fs, fn, pieces)
    cross = far_spectra(0, flag, sw, nw, u, fs, fn, fu, cross)
    own = regroup(to_lags(regroup(cross)))
    return assemble(lax.ppermute(own[:, 0], "pair", swap), lax.ppermute(own[:, 1], "pair", back))


def solution(mesh):
    return jax.shard_map(
        shards,
        mesh=mesh,
        in_specs=(P("band", None, None, "pair"), P(None, "pair")),
        out_specs=P(None, "band", "pair", None),
        check_vma=False,
    )
```

```python
import functools
import math

import jax
import jax.numpy as jnp
import numpy as np
from jax import lax
from jax.experimental import pallas as pl
from jax.experimental.pallas import tpu as pltpu
from jax.sharding import PartitionSpec as P

FREQS = 64
KEEP = 32
WIN = 384
EPSILON = 1e-06
BLOCK = 256
SUB = 16
STEP = 2
CUTS = (0, 6, 8)
VMEM_LIMIT = 28 * 1024 * 1024

BF16 = jnp.bfloat16
F32 = jnp.float32


def params():
    return pltpu.CompilerParams(vmem_limit_bytes=VMEM_LIMIT)


def lag_matrix(first, bins):
    lag_index = np.arange(KEEP, dtype=np.float32) - np.float32(KEEP // 2)
    bin_index = np.arange(FREQS, dtype=np.float32) + np.float32(1.0)
    step = np.float32(2.0 * math.pi / (2 * FREQS))
    phase = (step * lag_index)[:, None] * bin_index[None, :]
    table = np.stack([np.cos(phase), -np.sin(phase)], axis=2).reshape(KEEP, 8, 8, 2)
    table = table[:, :, first : first + bins].reshape(KEEP, 16 * bins)
    return jnp.asarray(np.kron(table, np.eye(SUB, dtype=np.float32)), dtype=BF16)


def whiten(raw, factor):
    if factor.dtype == BF16:
        return raw * factor[None]
    return (raw.astype(F32) * factor[None]).astype(BF16)


def product(left, right):
    windows = left.shape[1]
    rows = left.reshape(2 * windows, left.shape[2])
    top = jnp.concatenate([right[0], right[1]], axis=1)
    low = jnp.concatenate([right[1], -right[0]], axis=1)
    cols = jnp.concatenate([top, low], axis=0)
    return lax.dot_general(rows, cols, (((0,), (0,)), ((), ())), preferred_element_type=F32)


def store(out_ref, result):
    for part in range(2):
        piece = result[:, part * BLOCK : (part + 1) * BLOCK]
        out_ref[:, part] = piece.astype(BF16).reshape(8, 32, BLOCK)


def near_kernel(starts, odd_ref, s_ref, fs_ref, fn_ref, *refs):
    pieces, (sw_ref, nw_ref, out_ref) = refs[:-3], refs[-3:]
    step = pl.program_id(0)
    for index in range(STEP):
        f = step * STEP + index
        for n_ref, first, last in zip(pieces, starts, starts[1:]):

            @pl.when((step >= first // STEP) & (step < last // STEP))
            def _():
                nw_ref[f] = n_ref[index]

        sw_ref[f] = whiten(s_ref[f], fs_ref[...])

        @pl.when(odd_ref[0] != 0)
        def _():
            nw_ref[f] = whiten(nw_ref[f], fn_ref[...])
            store(out_ref.at[:, 2 * index : 2 * index + 2], product(nw_ref[f], sw_ref[f]))


def far_kernel(first, odd_ref, own_ref, near_ref, u_ref, fn_any, fu_any, _, out_ref, held_ref, fn_ref, fu_ref, send_ref, in_sem, factor_sem, out_sem):
    bins = u_ref.shape[0]
    odd = odd_ref[0]

    def fetch(f):
        return pltpu.make_async_copy(u_ref.at[f], held_ref.at[f], in_sem.at[f])

    def put(f, part):
        rows, columns = pl.ds(2 * f, 2), pl.ds(part * BLOCK, BLOCK)
        return pltpu.make_async_copy(
            send_ref.at[:, rows, :, columns],
            out_ref.at[:, pl.ds(2 * (first + f), 2), :, columns],
            out_sem.at[part, f],
        )

    def made(f, part, left, right):
        store(send_ref.at[:, pl.ds(2 * f, 2), :, pl.ds(part * BLOCK, BLOCK)], product(left, right))
        put(f, part).start()

    def factor(index):
        pairs = ((fu_any, fu_ref), (fn_any, fn_ref))
        return pltpu.make_async_copy(*pairs[index], factor_sem.at[index])

    factor(0).start()
    fetch(0).start()

    @pl.when(odd == 0)
    def _():
        factor(1).start()

    for f in range(1, bins):
        fetch(f).start()
    factor(0).wait()

    @pl.when(odd == 0)
    def _():
        factor(1).wait()

    def step(f, carry):
        fetch(f).wait()
        far = whiten(held_ref[f], fu_ref[...])

        @pl.when(odd == 0)
        def _():
            made(f, 0, whiten(near_ref[first + f], fn_ref[...]), far)
            made(f, 1, own_ref[first + f], far)

        @pl.when(odd != 0)
        def _():
            made(f, 1, far, own_ref[first + f])

        return carry

    lax.fori_loop(0, bins, step, 0, unroll=2)
    for f in range(bins):
        put(f, 1).wait()

    @pl.when(odd == 0)
    def _():
        for f in range(bins):
            put(f, 0).wait()


def flag_spec():
    return pl.BlockSpec(memory_space=pltpu.SMEM)


def held_spec():
    return pl.BlockSpec(memory_space=pltpu.VMEM)


SEND = (8, 16, 32, 2 * BLOCK)
SEND_BLOCK = (8, 2 * STEP, 32, BLOCK)
BINS_BLOCK = (STEP, 2, WIN, BLOCK)


def near_spectra(odd, s, fs, fn, pieces):
    shape = jax.ShapeDtypeStruct(s.shape, BF16)
    starts = [0]
    for piece in pieces:
        starts.append(starts[-1] + piece.shape[0])

    def piece_spec(first, last):
        return pl.BlockSpec(
            BINS_BLOCK, lambda g: (jnp.clip(g - first // STEP, 0, (last - first) // STEP - 1), 0, 0, 0)
        )

    return pl.pallas_call(
        functools.partial(near_kernel, starts),
        grid=(8 // STEP,),
        in_specs=[flag_spec(), held_spec(), held_spec(), held_spec()]
        + [piece_spec(first, last) for first, last in zip(starts, starts[1:])],
        out_specs=[held_spec(), held_spec(), pl.BlockSpec(SEND_BLOCK, lambda g: (0, g, 0, 0))],
        out_shape=[shape, shape, pltpu.HBM(SEND, BF16)],
        compiler_params=params(),
        cost_estimate=pl.CostEstimate(flops=0, bytes_accessed=0, transcendentals=0),
        name="near_spectra",
    )(odd, s, fs, fn, *pieces)


def far_spectra(first, odd, own, near, u, fn, fu, filled):
    bins = u.shape[0]
    anywhere = pl.BlockSpec(memory_space=pl.ANY)
    return pl.pallas_call(
        functools.partial(far_kernel, first),
        in_specs=[flag_spec(), held_spec(), held_spec()] + [anywhere] * 4,
        out_specs=anywhere,
        out_shape=pltpu.HBM(SEND, BF16),
        scratch_shapes=[
            pltpu.VMEM((bins, 2, WIN, BLOCK), BF16),
            pltpu.VMEM((WIN, BLOCK), fn.dtype),
            pltpu.VMEM((WIN, BLOCK), fu.dtype),
            pltpu.VMEM((8, 2 * bins, 32, 2 * BLOCK), BF16),
            pltpu.SemaphoreType.DMA((bins,)),
            pltpu.SemaphoreType.DMA((2,)),
            pltpu.SemaphoreType.DMA((2, bins)),
        ],
        input_output_aliases={6: 0},
        compiler_params=params(),
        cost_estimate=pl.CostEstimate(
            flops=bins * 2 * 2 * 768 * 256 * 512, bytes_accessed=bins << 20, transcendentals=0
        ),
        name="far" + str(first),
    )(odd, own, near, u, fn, fu, filled)


def lags_kernel(scale, matrix_ref, cross_ref, out_ref):
    for part in range(2):
        columns = slice(part * BLOCK, (part + 1) * BLOCK)
        cross = cross_ref[:, :, :, columns].reshape(2 * FREQS, 32, BLOCK)
        pair = jnp.concatenate([cross[:, :SUB], cross[:, SUB:]], axis=2)
        lagged = lax.dot_general(
            matrix_ref[...],
            pair.reshape(2 * FREQS * SUB, 2 * BLOCK),
            (((1,), (0,)), ((), ())),
            preferred_element_type=F32,
        )
        lagged = (lagged * scale).astype(BF16)
        for half in range(2):
            piece = lagged[:, half * BLOCK : (half + 1) * BLOCK].reshape(8, 4, SUB, BLOCK)
            out_ref[:, part, :, half * SUB : (half + 1) * SUB] = piece


def to_lags(cross):
    return pl.pallas_call(
        functools.partial(lags_kernel, 1.0 / math.sqrt(FREQS * WIN)),
        in_specs=[held_spec()] * 2,
        out_specs=held_spec(),
        out_shape=jax.ShapeDtypeStruct((8, 2, 4, 32, BLOCK), BF16),
        compiler_params=params(),
        cost_estimate=pl.CostEstimate(
            flops=2 * 512 * 2048 * 1024, bytes_accessed=7 << 20, transcendentals=0
        ),
        name="to_lags",
    )(lag_matrix(0, 8), cross)


def assemble_kernel(one_ref, two_ref, out_ref):
    for src in range(8):
        rows = slice(src * 32, src * 32 + 32)
        out_ref[0, :, rows] = one_ref[src]
        out_ref[1, :, rows] = two_ref[src]


def assemble(one, two):
    return pl.pallas_call(
        assemble_kernel,
        in_specs=[held_spec()] * 2,
        out_specs=held_spec(),
        out_shape=jax.ShapeDtypeStruct((2, 4, BLOCK, BLOCK), BF16),
        compiler_params=params(),
        cost_estimate=pl.CostEstimate(flops=0, bytes_accessed=2 << 20, transcendentals=0),
        name="assemble",
    )(one, two)


def exchange(value, partner):
    route = [(b, partner(b)) for b in range(8)]
    return lax.ppermute(value, "band", route)


def regroup(block):
    return lax.all_to_all(block, "band", split_axis=0, concat_axis=0, tiled=True)


def shards(spectra, window_valid):
    blocks = lax.axis_size("pair")
    flag = (lax.axis_index("pair") % 2).astype(jnp.int32).reshape(1)
    across = [((p + 2) % blocks, p) if p % 2 == 0 else ((p - 2) % blocks, p) for p in range(blocks)]
    swap = [(p ^ 1, p) for p in range(blocks)]
    back = [(p, p) if p % 2 == 0 else ((p + 2) % blocks, p) for p in range(blocks)]
    barrier = lax.optimization_barrier

    values = spectra.astype(F32)
    energy = jnp.sum(values * values, axis=(0, 1))
    pieces = [spectra[first:last] for first, last in zip(CUTS, CUTS[1:])]
    met, whole, pieces = barrier((exchange(energy.astype(BF16), lambda b: (b + 4) % 8), spectra, pieces))
    u = lax.ppermute(whole, "pair", across)
    pieces = [lax.ppermute(piece, "pair", swap) for piece in pieces]
    energy = energy + met.astype(F32)
    energy = energy + exchange(energy.astype(BF16), lambda b: b ^ 1).astype(F32)
    energy = energy + exchange(energy.astype(BF16), lambda b: (b // 4) * 4 + 3 - b % 4).astype(F32)
    fs = window_valid.astype(F32) * lax.rsqrt(energy / FREQS + EPSILON)
    fn = lax.ppermute(fs.astype(BF16), "pair", swap)
    fu = lax.ppermute(fs.astype(BF16), "pair", across)

    sw, nw, cross = near_spectra(flag, spectra, fs, fn, pieces)
    cross = far_spectra(0, flag, sw, nw, u, fn, fu, cross)
    own = regroup(to_lags(regroup(cross)))
    return assemble(lax.ppermute(own[:, 0], "pair", swap), lax.ppermute(own[:, 1], "pair", back))


def solution(mesh):
    return jax.shard_map(
        shards,
        mesh=mesh,
        in_specs=(P("band", None, None, "pair"), P(None, "pair")),
        out_specs=P(None, "band", "pair", None),
        check_vma=False,
    )
```
